256 devices in a mesh: orb: 16 (over x_lo, y, core), dom: 16 (over x_hi, z).
Axes of the slice: x: 4 (x_hi: 2, x_lo: 2; x = x_hi * 2 + x_lo), y: 4, z: 8, core: 2. Of those that a mesh axis runs over, the one named last changes fastest.
Arguments:
- orbitals: bfloat16 [128, 48, 4096], P('orb', 'dom'), may hold values from -6 to 6
- block_owner: int32 [1], replicated, may hold values from 0 to 15
Outputs:
- exchange_applied: bfloat16 [128, 48, 4096], P('orb', 'dom')
- intersection: float32 [128, 8], P('orb')
The draws below stay inside these ranges and needn't reach their ends.
Inputs may be any that keep to these rules, and one draw needn't show every extreme that they name: `block_owner`: one block index for the round.
All inputs are finite; a program needn't handle non-finite values.
Results may differ from the reference program's by a relative error of at most 0.003.
Values may be sent and summed in bfloat16 or wider, within the bound.
No kernel may reach another device: no remote copies, remote signals or barrier semaphores. Data moves between devices by JAX's collectives and lax.ppermute only.
A program may use at most 128 MiB of HBM per device.

```python
import jax
import jax.numpy as jnp
from jax import lax

NX = 64
NY = 64
OWN = 8
BLK = 8
SWEEPS = 4
PLANE = 4096
NZ = 48
ORBS = 128
NBLOCKS = 16
N_ORB = 16


def block_levels(rng, dims, split, smallest, high):
    level, own = 1.0, jax.random.fold_in(rng, 6)
    for dim, shards_of in split:
        heights = jnp.exp(jax.random.uniform(jax.random.fold_in(own, dim), (shards_of,), jnp.float32, smallest / len(split), high / len(split)))
        level = level * jnp.repeat(heights, dims[dim] // shards_of).reshape([-1 if axis == dim else 1 for axis in range(len(dims))])
    return level


def normal_values(rng, shape, scale, bound, cuts=(), held_as=jnp.bfloat16):
    loudness = block_levels(rng, shape, cuts, -0.22, 0.18) if cuts else 1.0
    result = jax.random.normal(rng, shape, jnp.float32) * scale * loudness
    return jnp.minimum(jnp.maximum(result, -bound), bound).astype(held_as)


def setup_inputs(seed: int = 0) -> dict:
    streams_of = jax.random.split(jax.random.key(seed), 3)
    orbitals = normal_values(streams_of[0], (ORBS, NZ, PLANE), 1.0, 6.0, ((0, 16), (1, 16)))
    block_owner = jax.random.randint(streams_of[1], (1,), 0, NBLOCKS).astype(jnp.int32)
    return dict(orbitals=orbitals, block_owner=block_owner)


inv_diag = 1.0 / 6.02


def neighbours(field):
    total = jnp.roll(field, 1, -1) + jnp.roll(field, -1, -1)
    total = total + jnp.roll(field, 1, -2) + jnp.roll(field, -1, -2)
    return total + jnp.roll(field, 1, -3) + jnp.roll(field, -1, -3)


def reference(orbitals, block_owner):
    grid = orbitals.reshape(ORBS, NZ, NX, NY)
    start = (block_owner[0] * BLK).astype(jnp.int32)
    phi = lax.dynamic_slice_in_dim(grid, start, BLK, 0).astype(jnp.float32)

    def one_group(group):
        own = lax.dynamic_slice_in_dim(grid, (group * OWN).astype(jnp.int32), OWN, 0)
        ownf = own.astype(jnp.float32)
        rho = phi[:, None] * ownf[None, :]
        pot = rho * inv_diag
        for sweep in range(SWEEPS - 1):
            pot = (rho + neighbours(pot)) * inv_diag
        applied = (-jnp.sum(pot * phi[:, None], axis=0)).astype(jnp.bfloat16)
        flat_own = own.reshape(OWN, NZ * PLANE)
        flat_app = applied.reshape(OWN, NZ * PLANE)
        prod = lax.dot_general(flat_own, flat_app, (((1,), (1,)), ((), ())), preferred_element_type=jnp.float32) / 512.0
        return applied, prod

    applied, prod = lax.map(one_group, jnp.arange(N_ORB, dtype=jnp.int32))
    return applied.reshape(ORBS, NZ, PLANE), prod.reshape(ORBS, OWN)
```

```python
import itertools

import jax
import jax.numpy as jnp
from jax import lax
from jax.experimental import pallas as pl
from jax.experimental.pallas import tpu as pltpu
from jax.sharding import PartitionSpec as P

NY = 64
OWN = 8
LANES = 128
ROWS = 32
PAD = 2
DEPTH = 3
REACH = 3

C = 1.0 / 6.02


def weight(dx, dy, dz):
    steps = ((1, 0, 0), (-1, 0, 0), (0, 1, 0), (0, -1, 0), (0, 0, 1), (0, 0, -1))
    total = 0.0
    for length in range(REACH + 1):
        walks = sum(
            tuple(map(sum, zip((0, 0, 0), *walk))) == (dx, dy, dz)
            for walk in itertools.product(steps, repeat=length)
        )
        total += walks * C ** (length + 1)
    return total


WEIGHTS = {
    d: weight(*d)
    for d in itertools.product(range(REACH + 1), repeat=3)
    if sum(d) <= REACH
}


def spread_matrix():
    row = lax.broadcasted_iota(jnp.int32, (LANES, 2 * LANES), 0)
    col = lax.broadcasted_iota(jnp.int32, (LANES, 2 * LANES), 1)
    half = col // LANES
    lane = col % LANES
    source = (lane % 2 + half) % 2 * NY + lane // 2
    return jnp.where(row == source, 1.0, 0.0).astype(jnp.bfloat16)


def gather_matrix():
    row = lax.broadcasted_iota(jnp.int32, (LANES, LANES), 0)
    col = lax.broadcasted_iota(jnp.int32, (LANES, LANES), 1)
    source = col % NY * 2 + col // NY
    return jnp.where(row == source, 1.0, 0.0).astype(jnp.bfloat16)


def kernel(phi_m, phi_0, phi_p, orb_m, orb_0, orb_p, out, part, fa, fb, oa, ob, acc):
    spread = spread_matrix()
    odd = lax.broadcasted_iota(jnp.int32, (ROWS * OWN, LANES), 1) % 2 == 1

    def lay_out(source, even_ref, odd_ref, plane):
        wide = source.astype(jnp.float32)
        tall = jnp.concatenate(
            [wide[:, r * LANES : (r + 1) * LANES] for r in range(ROWS)], axis=0
        )
        both = jnp.dot(
            tall.astype(jnp.bfloat16), spread, preferred_element_type=jnp.float32
        )
        a, b = both[:, :LANES], both[:, LANES:]
        b = jnp.where(odd, jnp.concatenate([b[OWN:], b[:OWN]], axis=0), b)
        n, p = ROWS * OWN, PAD * OWN
        for ref, value in ((even_ref, a), (odd_ref, b)):
            ref[plane, p : p + n] = value
            ref[plane, :p] = value[n - p :]
            ref[plane, p + n :] = value[:p]

    for block, (f, o) in enumerate(((phi_m, orb_m), (phi_0, orb_0), (phi_p, orb_p))):
        for z in range(DEPTH):
            lay_out(f[z], fa, fb, block * DEPTH + z)
            lay_out(o[z], oa, ob, block * DEPTH + z)

    def plane_step(z, carry):
        for tile in range(ROWS // 8):

            def read(refs, dx, dz, i):
                ref, k = refs[dx % 2], dx // 2
                start = (tile * 8 + PAD + k) * OWN + i
                return ref[z + (DEPTH + dz), pl.ds(start, 8, stride=OWN), :]

            total = [None] * OWN
            for dy in range(-REACH, REACH + 1):
                here = [read((fa, fb), 0, 0, i) for i in range(OWN)]
                if dy:
                    here = [pltpu.roll(v, 2 * dy % LANES, 1) for v in here]
                sums = [None] * OWN
                rest = REACH - abs(dy)
                for dz in range(-rest, rest + 1):
                    for dx in range(abs(dz) - rest, rest - abs(dz) + 1):
                        g = None
                        for i in range(OWN):
                            term = here[i] * read((fa, fb), dx, dz, i)
                            g = term if g is None else g + term
                        g = g * (-WEIGHTS[abs(dx), abs(dy), abs(dz)])
                        for j in range(OWN):
                            term = g * read((oa, ob), dx, dz, j)
                            sums[j] = term if sums[j] is None else sums[j] + term
                for j in range(OWN):
                    s = pltpu.roll(sums[j], -2 * dy % LANES, 1) if dy else sums[j]
                    total[j] = s if total[j] is None else total[j] + s
            for j in range(OWN):
                acc[z, pl.ds(tile * 8 * OWN + j, 8, stride=OWN), :] = total[j]
        return carry

    lax.fori_loop(0, DEPTH, plane_step, 0)

    gather = gather_matrix()
    products = None
    for z in range(DEPTH):
        tall = jnp.dot(
            acc[z].astype(jnp.bfloat16), gather, preferred_element_type=jnp.float32
        )
        wide = jnp.concatenate(
            [tall[r * OWN : (r + 1) * OWN] for r in range(ROWS)], axis=1
        ).astype(jnp.bfloat16)
        out[z] = wide
        term = lax.dot_general(
            orb_0[z], wide, (((1,), (1,)), ((), ())), preferred_element_type=jnp.float32
        )
        products = term if products is None else products + term
    part[...] = products


def apply_exchange(phis, orbs):
    rows = (ROWS + 2 * PAD) * OWN
    field = pltpu.VMEM((3 * DEPTH, rows, LANES), jnp.float32)
    return pl.pallas_call(
        kernel,
        out_shape=(
            jax.ShapeDtypeStruct((DEPTH, OWN, ROWS * LANES), jnp.bfloat16),
            jax.ShapeDtypeStruct((OWN, OWN), jnp.float32),
        ),
        in_specs=[pl.BlockSpec(memory_space=pltpu.VMEM)] * 6,
        out_specs=[pl.BlockSpec(memory_space=pltpu.VMEM)] * 2,
        scratch_shapes=[field] * 4
        + [pltpu.VMEM((DEPTH, ROWS * OWN, LANES), jnp.float32)],
        compiler_params=pltpu.CompilerParams(vmem_limit_bytes=40 * 1024 * 1024),
        cost_estimate=pl.CostEstimate(
            flops=50_000_000, bytes_accessed=2_000_000, transcendentals=0
        ),
    )(*phis, *orbs)


def halo(x, pairs_of):
    return lax.ppermute(x, ("orb", "dom"), pairs_of(1)), lax.ppermute(
        x, ("orb", "dom"), pairs_of(-1)
    )


def slab_pairs(groups, count):
    return lambda step: [
        (g * count + s, g * count + (s + step) % count)
        for g in groups
        for s in range(count)
    ]


def phi_from(owner, count, x):
    me = lax.axis_index("orb")
    have = [owner]
    buf = jnp.where(me == owner, x, 0)
    for bit in (2, 6, 8):
        buf = buf + lax.ppermute(buf, "orb", [(h, h ^ bit) for h in have])
        have = have + [h ^ bit for h in have]
    low, high = halo(buf, slab_pairs(have, count))
    full = jnp.concatenate([low, buf, high], axis=0)
    return full + lax.ppermute(full, "orb", [(h, h ^ 1) for h in range(16)])


def on_device(orbitals, block_owner):
    count = lax.axis_size("dom")
    groups = lax.axis_size("orb")
    x = jnp.transpose(orbitals, (1, 0, 2))
    low, high = halo(x, slab_pairs(range(groups), count))
    phi = lax.switch(
        block_owner[0],
        [lambda v, w=w: phi_from(w, count, v) for w in range(groups)],
        x,
    )
    phis = (phi[:DEPTH], phi[DEPTH : 2 * DEPTH], phi[2 * DEPTH :])
    applied, total = apply_exchange(phis, (low, x, high))
    for bits in (1, 3, 6, 8):
        total = total + lax.ppermute(
            total, "dom", [(s, s ^ bits) for s in range(count)]
        )
    return jnp.transpose(applied, (1, 0, 2)), total / 512.0


def solution(mesh):
    in_specs = (P("orb", "dom", None), P())
    out_specs = (P("orb", "dom", None), P("orb", None))
    return jax.shard_map(
        on_device, mesh=mesh, in_specs=in_specs, out_specs=out_specs, check_vma=False
    )
```

```python
import itertools

import jax
import jax.numpy as jnp
from jax import lax
from jax.experimental import pallas as pl
from jax.experimental.pallas import tpu as pltpu
from jax.sharding import PartitionSpec as P

NY = 64
OWN = 8
LANES = 128
ROWS = 32
PAD = 2
DEPTH = 3
REACH = 3

C = 1.0 / 6.02


def weight(dx, dy, dz):
    steps = ((1, 0, 0), (-1, 0, 0), (0, 1, 0), (0, -1, 0), (0, 0, 1), (0, 0, -1))
    total = 0.0
    for length in range(REACH + 1):
        walks = sum(
            tuple(map(sum, zip((0, 0, 0), *walk))) == (dx, dy, dz)
            for walk in itertools.product(steps, repeat=length)
        )
        total += walks * C ** (length + 1)
    return total


WEIGHTS = {
    d: weight(*d)
    for d in itertools.product(range(REACH + 1), repeat=3)
    if sum(d) <= REACH
}


def spread_matrix():
    row = lax.broadcasted_iota(jnp.int32, (LANES, 2 * LANES), 0)
    col = lax.broadcasted_iota(jnp.int32, (LANES, 2 * LANES), 1)
    half = col // LANES
    lane = col % LANES
    source = (lane % 2 + half) % 2 * NY + lane // 2
    return jnp.where(row == source, 1.0, 0.0).astype(jnp.bfloat16)


def gather_matrix():
    row = lax.broadcasted_iota(jnp.int32, (LANES, LANES), 0)
    col = lax.broadcasted_iota(jnp.int32, (LANES, LANES), 1)
    source = col % NY * 2 + col // NY
    return jnp.where(row == source, 1.0, 0.0).astype(jnp.bfloat16)


def lay_out(source, spread):
    wide = source.astype(jnp.float32)
    count = wide.shape[1] // LANES
    tall = jnp.concatenate(
        [wide[:, r * LANES : (r + 1) * LANES] for r in range(count)], axis=0
    )
    both = jnp.dot(
        tall.astype(jnp.bfloat16), spread, preferred_element_type=jnp.float32
    )
    return both[:, :LANES], both[:, LANES:]


def finish_plane(even, swapped, even_ref, odd_ref, plane):
    lane = lax.broadcasted_iota(jnp.int32, (ROWS * OWN, LANES), 1)
    ahead = jnp.concatenate([swapped[OWN:], swapped[:OWN]], axis=0)
    odd = jnp.where(lane % 2 == 1, ahead, swapped)
    n, p = ROWS * OWN, PAD * OWN
    for ref, value in ((even_ref, even), (odd_ref, odd)):
        ref[plane, p : p + n] = value
        ref[plane, :p] = value[n - p :]
        ref[plane, p + n :] = value[:p]


def put_whole(source, spread, even_ref, odd_ref, plane):
    finish_plane(*lay_out(source, spread), even_ref, odd_ref, plane)


def put_halves(core, mine, other, spread, even_ref, odd_ref, plane):
    a, b = lay_out(mine, spread), lay_out(other, spread)
    first = [jnp.where(core == 0, s, t) for s, t in zip(a, b)]
    second = [jnp.where(core == 0, t, s) for s, t in zip(a, b)]
    both = [jnp.concatenate(pair, axis=0) for pair in zip(first, second)]
    finish_plane(*both, even_ref, odd_ref, plane)


def add_planes(pairs, phi, orb, acc_in, acc_out, here_plane):
    def tile_step(tile, carry):
        def read(field, z, dx, i):
            refs, plane = field(z)
            start = tile * (8 * OWN) + (PAD + dx // 2) * OWN + i
            return refs[dx % 2][plane, pl.ds(start, 8, stride=OWN), :]

        for z in range(DEPTH):
            if acc_in is None:
                total = [None] * OWN
            else:
                total = [
                    acc_in[z, pl.ds(tile * (8 * OWN) + j, 8, stride=OWN), :]
                    for j in range(OWN)
                ]
            centre = [read(here_plane, z, 0, i) for i in range(OWN)]
            for reach in range(REACH + 1):
                signs = (reach, -reach) if reach else (0,)
                here = [
                    [pltpu.roll(v, 2 * dy % LANES, 1) if dy else v for v in centre]
                    for dy in signs
                ]
                sums = [[None] * OWN for _ in signs]
                rest = REACH - reach
                for dz in range(-rest, rest + 1):
                    if (z, dz) not in pairs:
                        continue
                    for dx in range(abs(dz) - rest, rest - abs(dz) + 1):
                        g = [None for _ in signs]
                        for i in range(OWN):
                            there = read(phi, z + dz, dx, i)
                            for s in range(len(signs)):
                                term = here[s][i] * there
                                g[s] = term if g[s] is None else g[s] + term
                        scale = -WEIGHTS[abs(dx), reach, abs(dz)]
                        g = [v * scale for v in g]
                        for j in range(OWN):
                            there = read(orb, z + dz, dx, j)
                            for s in range(len(signs)):
                                term = g[s] * there
                                old = sums[s][j]
                                sums[s][j] = term if old is None else old + term
                for s, dy in enumerate(signs):
                    for j in range(OWN):
                        term = sums[s][j]
                        if term is None:
                            continue
                        if dy:
                            term = pltpu.roll(term, -2 * dy % LANES, 1)
                        total[j] = term if total[j] is None else total[j] + term
            for j in range(OWN):
                acc_out[z, pl.ds(tile * (8 * OWN) + j, 8, stride=OWN), :] = total[j]
        return carry

    lax.fori_loop(0, ROWS // 8, tile_step, 0)


INSIDE = [
    (z, dz)
    for z in range(DEPTH)
    for dz in range(-REACH, REACH + 1)
    if 0 <= z + dz < DEPTH
]
OUTSIDE = [
    (z, dz)
    for z in range(DEPTH)
    for dz in range(-REACH, REACH + 1)
    if not 0 <= z + dz < DEPTH
]


def inner_kernel(core, mine, other, own, acc, fa, fb, oa, ob):
    spread = spread_matrix()
    for z in range(DEPTH):
        put_halves(core[0], mine[z], other[z], spread, fa, fb, z)
        put_whole(own[z], spread, oa, ob, z)
    phi = lambda z: ((fa, fb), z)
    orb = lambda z: ((oa, ob), z)
    add_planes(INSIDE, phi, orb, None, acc, phi)


def outer_kernel(
    core, mine, other, far_mine, far_other, low, own, high, acc_in,
    out, part, here, fa, fb, oa, ob, acc,
):
    spread = spread_matrix()
    for z in range(DEPTH):
        a, b = lay_out(mine[z], spread)[0], lay_out(other[z], spread)[0]
        n = a.shape[0]
        here[z, PAD * OWN : PAD * OWN + n] = jnp.where(core[0] == 0, a, b)
        here[z, PAD * OWN + n : PAD * OWN + 2 * n] = jnp.where(core[0] == 0, b, a)
        put_whole(low[z], spread, oa, ob, z)
        put_whole(high[z], spread, oa, ob, DEPTH + z)
    for z in range(2 * DEPTH):
        put_halves(core[0], far_mine[z], far_other[z], spread, fa, fb, z)
    place = lambda z: z + DEPTH if z < 0 else z
    phi = lambda z: ((fa, fb), place(z))
    orb = lambda z: ((oa, ob), place(z))
    add_planes(OUTSIDE, phi, orb, acc_in, acc, lambda z: ((here,), z))

    gather = gather_matrix()
    products = None
    for z in range(DEPTH):
        tall = jnp.dot(
            acc[z].astype(jnp.bfloat16), gather, preferred_element_type=jnp.float32
        )
        wide = jnp.concatenate(
            [tall[r * OWN : (r + 1) * OWN] for r in range(ROWS)], axis=1
        ).astype(jnp.bfloat16)
        out[z] = wide
        term = lax.dot_general(
            own[z], wide, (((1,), (1,)), ((), ())), preferred_element_type=jnp.float32
        )
        products = term if products is None else products + term
    part[...] = products


def field(planes):
    return pltpu.VMEM((planes, (ROWS + 2 * PAD) * OWN, LANES), jnp.float32)


SUMS = (DEPTH, ROWS * OWN, LANES)
ON_CHIP = pl.BlockSpec(memory_space=pltpu.VMEM)
SCALAR = pl.BlockSpec(memory_space=pltpu.SMEM)
PARAMS = pltpu.CompilerParams(vmem_limit_bytes=32 * 1024 * 1024)


def inner(core, mine, other, own):
    return pl.pallas_call(
        inner_kernel,
        out_shape=jax.ShapeDtypeStruct(SUMS, jnp.float32),
        in_specs=[SCALAR] + [ON_CHIP] * 3,
        out_specs=ON_CHIP,
        scratch_shapes=[field(DEPTH)] * 4,
        compiler_params=PARAMS,
        cost_estimate=pl.CostEstimate(
            flops=40_000_000, bytes_accessed=1_000_000, transcendentals=0
        ),
    )(core, mine, other, own)


def outer(core, mine, other, far_mine, far_other, low, own, high, acc):
    return pl.pallas_call(
        outer_kernel,
        out_shape=(
            jax.ShapeDtypeStruct((DEPTH, OWN, ROWS * LANES), jnp.bfloat16),
            jax.ShapeDtypeStruct((OWN, OWN), jnp.float32),
        ),
        in_specs=[SCALAR] + [ON_CHIP] * 8,
        out_specs=[ON_CHIP] * 2,
        scratch_shapes=[field(DEPTH)]
        + [field(2 * DEPTH)] * 4
        + [pltpu.VMEM(SUMS, jnp.float32)],
        compiler_params=PARAMS,
        cost_estimate=pl.CostEstimate(
            flops=20_000_000, bytes_accessed=2_000_000, transcendentals=0
        ),
    )(core, mine, other, far_mine, far_other, low, own, high, acc)


def shift_pairs(count, step):
    return [(s, (s + step) % count) for s in range(count)]


def halo(x):
    count = lax.axis_size("dom")
    low = lax.ppermute(x, "dom", shift_pairs(count, 1))
    return low, lax.ppermute(x, "dom", shift_pairs(count, -1))


def swap(x, axis, bits):
    return lax.ppermute(x, axis, [(i, i ^ bits) for i in range(lax.axis_size(axis))])


def on_device(orbitals, block_owner):
    x = jnp.transpose(orbitals, (1, 0, 2))
    me = lax.axis_index("orb")
    core = me % 2
    half = x.shape[2] // 2
    cut = lambda v: lax.dynamic_slice_in_dim(v, core * half, half, 2)
    low, high = halo(x)
    from_mate = swap(x, "orb", 1)
    zero = jnp.zeros((), x.dtype)
    mine = jnp.where(me == block_owner[0], cut(x), zero)
    mine = jnp.where(me ^ 1 == block_owner[0], cut(from_mate), mine)
    for bits in (8, 2, 6):
        mine = mine + swap(mine, "orb", bits)
    low, high, mine = lax.optimization_barrier((low, high, mine))
    far = halo(mine)
    other = swap(mine, "orb", 1)
    index = core.reshape(1)
    acc = inner(index, mine, other, x)
    far_mine = jnp.concatenate(far, axis=0)
    far_other = swap(far_mine, "orb", 1)
    applied, total = outer(
        index, mine, other, far_mine, far_other, low, x, high, acc
    )
    for group in ((1, 2, 3), (6, 8, 14)):
        total = sum([swap(total, "dom", bits) for bits in group], total)
    return jnp.transpose(applied, (1, 0, 2)), total / 512.0


def solution(mesh):
    in_specs = (P("orb", "dom", None), P())
    out_specs = (P("orb", "dom", None), P("orb", None))
    return jax.shard_map(
        on_device, mesh=mesh, in_specs=in_specs, out_specs=out_specs, check_vma=False
    )
```

```python
import itertools

import jax
import jax.numpy as jnp
from jax import lax
from jax.experimental import pallas as pl
from jax.experimental.pallas import tpu as pltpu
from jax.sharding import PartitionSpec as P

NY = 64
OWN = 8
LANES = 128
CELLS = 4096
ROWS = 32
PAD = 2
DEPTH = 3
REACH = 3

C = 1.0 / 6.02


def weight(dx, dy, dz):
    steps = ((1, 0, 0), (-1, 0, 0), (0, 1, 0), (0, -1, 0), (0, 0, 1), (0, 0, -1))
    total = 0.0
    for length in range(REACH + 1):
        walks = sum(
            tuple(map(sum, zip((0, 0, 0), *walk))) == (dx, dy, dz)
            for walk in itertools.product(steps, repeat=length)
        )
        total += walks * C ** (length + 1)
    return total


WEIGHTS = {
    d: weight(*d)
    for d in itertools.product(range(REACH + 1), repeat=3)
    if sum(d) <= REACH
}


def spread_matrix():
    row = lax.broadcasted_iota(jnp.int32, (LANES, 2 * LANES), 0)
    col = lax.broadcasted_iota(jnp.int32, (LANES, 2 * LANES), 1)
    half = col // LANES
    lane = col % LANES
    source = (lane % 2 + half) % 2 * NY + lane // 2
    return jnp.where(row == source, 1.0, 0.0).astype(jnp.bfloat16)


def gather_matrix():
    row = lax.broadcasted_iota(jnp.int32, (LANES, LANES), 0)
    col = lax.broadcasted_iota(jnp.int32, (LANES, LANES), 1)
    source = col % NY * 2 + col // NY
    return jnp.where(row == source, 1.0, 0.0).astype(jnp.bfloat16)


def lay_out(source, spread):
    wide = source.astype(jnp.float32)
    count = wide.shape[1] // LANES
    tall = jnp.concatenate(
        [wide[:, r * LANES : (r + 1) * LANES] for r in range(count)], axis=0
    )
    both = jnp.dot(
        tall.astype(jnp.bfloat16), spread, preferred_element_type=jnp.float32
    )
    return both[:, :LANES], both[:, LANES:]


def finish_plane(even, swapped, even_ref, odd_ref, plane):
    lane = lax.broadcasted_iota(jnp.int32, (ROWS * OWN, LANES), 1)
    ahead = jnp.concatenate([swapped[OWN:], swapped[:OWN]], axis=0)
    odd = jnp.where(lane % 2 == 1, ahead, swapped)
    n, p = ROWS * OWN, PAD * OWN
    for ref, value in ((even_ref, even), (odd_ref, odd)):
        ref[plane, p : p + n] = value
        ref[plane, :p] = value[n - p :]
        ref[plane, p + n :] = value[:p]


def put_whole(source, spread, even_ref, odd_ref, plane):
    finish_plane(*lay_out(source, spread), even_ref, odd_ref, plane)


def whole(core, mine, other):
    return jnp.concatenate(
        [jnp.where(core == 0, mine, other), jnp.where(core == 0, other, mine)], axis=1
    )


def add_planes(pairs, phi, orb, acc_in, acc_out, here_plane):
    def tile_step(tile, carry):
        def read(field, z, dx, i):
            refs, plane = field(z)
            start = tile * (8 * OWN) + (PAD + dx // 2) * OWN + i
            return refs[dx % 2][plane, pl.ds(start, 8, stride=OWN), :]

        for z in range(DEPTH):
            if acc_in is None:
                total = [None] * OWN
            else:
                total = [
                    acc_in[z, pl.ds(tile * (8 * OWN) + j, 8, stride=OWN), :]
                    for j in range(OWN)
                ]
            centre = [read(here_plane, z, 0, i) for i in range(OWN)]
            for reach in range(REACH + 1):
                signs = (reach, -reach) if reach else (0,)
                here = [
                    [pltpu.roll(v, 2 * dy % LANES, 1) if dy else v for v in centre]
                    for dy in signs
                ]
                sums = [[None] * OWN for _ in signs]
                rest = REACH - reach
                for dz in range(-rest, rest + 1):
                    if (z, dz) not in pairs:
                        continue
                    for dx in range(abs(dz) - rest, rest - abs(dz) + 1):
                        g = [None for _ in signs]
                        for i in range(OWN):
                            there = read(phi, z + dz, dx, i)
                            for s in range(len(signs)):
                                term = here[s][i] * there
                                g[s] = term if g[s] is None else g[s] + term
                        scale = -WEIGHTS[abs(dx), reach, abs(dz)]
                        g = [v * scale for v in g]
                        for j in range(OWN):
                            there = read(orb, z + dz, dx, j)
                            for s in range(len(signs)):
                                term = g[s] * there
                                old = sums[s][j]
                                sums[s][j] = term if old is None else old + term
                for s, dy in enumerate(signs):
                    for j in range(OWN):
                        term = sums[s][j]
                        if term is None:
                            continue
                        if dy:
                            term = pltpu.roll(term, -2 * dy % LANES, 1)
                        total[j] = term if total[j] is None else total[j] + term
            for j in range(OWN):
                acc_out[z, pl.ds(tile * (8 * OWN) + j, 8, stride=OWN), :] = total[j]
        return carry

    lax.fori_loop(0, ROWS // 8, tile_step, 0)


INSIDE = [
    (z, dz)
    for z in range(DEPTH)
    for dz in range(-REACH, REACH + 1)
    if 0 <= z + dz < DEPTH
]
OUTSIDE = [
    (z, dz)
    for z in range(DEPTH)
    for dz in range(-REACH, REACH + 1)
    if not 0 <= z + dz < DEPTH
]


def kind_of(index):
    return (index ^ (index >> 1) ^ (index >> 3)) & 1


def inner_kernel(mine, other, own, acc, fa, fb, oa, ob):
    spread = spread_matrix()
    kind = kind_of(lax.axis_index("orb"))
    for z in range(DEPTH):
        put_whole(whole(kind, mine[z], other[z]), spread, fa, fb, z)
        put_whole(own[z], spread, oa, ob, z)
    phi = lambda z: ((fa, fb), z)
    orb = lambda z: ((oa, ob), z)
    add_planes(INSIDE, phi, orb, None, acc, phi)


def outer_kernel(
    mine, other, first, second, first_mine, second_mine, first_other, second_other,
    own, acc_in,
    out, part, here, fa, fb, oa, ob, acc,
):
    spread = spread_matrix()
    core = kind_of(lax.axis_index("orb"))
    base = first_is_above(lax.axis_index("orb"), lax.axis_index("dom")) * DEPTH
    rest = DEPTH - base
    for z in range(DEPTH):
        centre = lay_out(whole(core, mine[z], other[z]), spread)[0]
        here[z, PAD * OWN : (PAD + ROWS) * OWN] = centre
        for orbs, halves, plane in (
            (first, (first_mine, first_other), base + z),
            (second, (second_mine, second_other), rest + z),
        ):
            phis = whole(core, halves[0][z], halves[1][z])
            put_whole(orbs[z], spread, oa, ob, plane)
            put_whole(phis, spread, fa, fb, plane)
    plane_of = lambda z: z + DEPTH if z < 0 else z
    phi = lambda z: ((fa, fb), plane_of(z))
    orb = lambda z: ((oa, ob), plane_of(z))
    add_planes(OUTSIDE, phi, orb, acc_in, acc, lambda z: ((here,), z))

    gather = gather_matrix()
    products = None
    for z in range(DEPTH):
        tall = jnp.dot(
            acc[z].astype(jnp.bfloat16), gather, preferred_element_type=jnp.float32
        )
        wide = jnp.concatenate(
            [tall[r * OWN : (r + 1) * OWN] for r in range(ROWS)], axis=1
        ).astype(jnp.bfloat16)
        out[z] = wide
        term = lax.dot_general(
            own[z], wide, (((1,), (1,)), ((), ())), preferred_element_type=jnp.float32
        )
        products = term if products is None else products + term
    part[...] = products


def field(planes):
    return pltpu.VMEM((planes, (ROWS + 2 * PAD) * OWN, LANES), jnp.float32)


SUMS = (DEPTH, ROWS * OWN, LANES)
ON_CHIP = pl.BlockSpec(memory_space=pltpu.VMEM)
PARAMS = pltpu.CompilerParams(vmem_limit_bytes=32 * 1024 * 1024)


def inner(mine, other, own):
    return pl.pallas_call(
        inner_kernel,
        out_shape=jax.ShapeDtypeStruct(SUMS, jnp.float32),
        in_specs=[ON_CHIP] * 3,
        out_specs=ON_CHIP,
        scratch_shapes=[field(DEPTH)] * 4,
        compiler_params=PARAMS,
        cost_estimate=pl.CostEstimate(
            flops=40_000_000, bytes_accessed=1_000_000, transcendentals=0
        ),
    )(mine, other, own)


def outer(*parts):
    return pl.pallas_call(
        outer_kernel,
        out_shape=(
            jax.ShapeDtypeStruct((DEPTH, OWN, ROWS * LANES), jnp.bfloat16),
            jax.ShapeDtypeStruct((OWN, OWN), jnp.float32),
        ),
        in_specs=[ON_CHIP] * 10,
        out_specs=[ON_CHIP] * 2,
        scratch_shapes=[field(DEPTH)]
        + [field(2 * DEPTH)] * 4
        + [pltpu.VMEM(SUMS, jnp.float32)],
        compiler_params=PARAMS,
        cost_estimate=pl.CostEstimate(
            flops=20_000_000, bytes_accessed=2_000_000, transcendentals=0
        ),
    )(*parts)


def swap(x, axis, bits_of):
    size = lax.axis_size(axis)
    return lax.ppermute(x, axis, [(i, i ^ bits_of(i)) for i in range(size)])


def first_is_above(orb, dom):
    return (dom + (orb >> 3)) & 1


def swap_slabs(x):
    axes = ("orb", "dom")
    groups, count = map(lax.axis_size, axes)

    def swap_one(first):
        pairs = []
        for g, s in itertools.product(range(groups), range(count)):
            up = first_is_above(g, s) == first
            target = (s + (1 if up else -1)) % count
            pairs.append((g * count + s, g * count + target))
        return lax.ppermute(x, axes, pairs)

    return swap_one(True), swap_one(False)


def on_device(orbitals, block_owner):
    x = jnp.transpose(orbitals, (1, 0, 2))
    me = lax.axis_index("orb")
    owner = block_owner[0]
    kind = kind_of(me)
    half = x.shape[2] // 2
    cut = lambda v: jnp.where(kind == 0, v[:, :, :half], v[:, :, half:])
    first, second = swap_slabs(x)
    from_mate = swap(x, "orb", lambda i: 1)
    mine = jnp.where(me == owner, cut(x), cut(from_mate))
    known = 1
    for by_kind in ((8, 2), (2, 6), (6, 8)):
        theirs = swap(mine, "orb", lambda i: by_kind[kind_of(i)] ^ 1)
        have = (me ^ owner) & ~known == 0
        mine = jnp.where(have, mine, theirs)
        known = known | jnp.where(kind == 0, by_kind[0], by_kind[1])
    far = swap_slabs(mine)
    other = swap(mine, "orb", lambda i: 1)
    acc = inner(mine, other, x)
    *far, acc, first, second = lax.optimization_barrier((*far, acc, first, second))
    others = [swap(v, "orb", lambda i: 1) for v in far]
    applied, total = outer(mine, other, first, second, *far, *others, x, acc)
    total = lax.all_to_all(
        jnp.broadcast_to(total[None], (lax.axis_size("dom"), OWN, OWN)), "dom", 0, 0
    ).sum(0)
    return jnp.transpose(applied, (1, 0, 2)), total / 512.0


def solution(mesh):
    in_specs = (P("orb", "dom", None), P())
    out_specs = (P("orb", "dom", None), P("orb", None))
    return jax.shard_map(
        on_device, mesh=mesh, in_specs=in_specs, out_specs=out_specs, check_vma=False
    )
```

```python
import itertools

import jax
import jax.numpy as jnp
from jax import lax
from jax.experimental import pallas as pl
from jax.experimental.pallas import tpu as pltpu
from jax.sharding import PartitionSpec as P

NY = 64
OWN = 8
LANES = 128
CELLS = 4096
ROWS = 32
PAD = 2
DEPTH = 3
REACH = 3

C = 1.0 / 6.02


def weight(dx, dy, dz):
    steps = ((1, 0, 0), (-1, 0, 0), (0, 1, 0), (0, -1, 0), (0, 0, 1), (0, 0, -1))
    total = 0.0
    for length in range(REACH + 1):
        walks = sum(
            tuple(map(sum, zip((0, 0, 0), *walk))) == (dx, dy, dz)
            for walk in itertools.product(steps, repeat=length)
        )
        total += walks * C ** (length + 1)
    return total


WEIGHTS = {
    d: weight(*d)
    for d in itertools.product(range(REACH + 1), repeat=3)
    if sum(d) <= REACH
}


def spread_matrix():
    row = lax.broadcasted_iota(jnp.int32, (LANES, 2 * LANES), 0)
    col = lax.broadcasted_iota(jnp.int32, (LANES, 2 * LANES), 1)
    half = col // LANES
    lane = col % LANES
    source = (lane % 2 + half) % 2 * NY + lane // 2
    return jnp.where(row == source, 1.0, 0.0).astype(jnp.bfloat16)


def gather_matrix():
    row = lax.broadcasted_iota(jnp.int32, (LANES, LANES), 0)
    col = lax.broadcasted_iota(jnp.int32, (LANES, LANES), 1)
    source = col % NY * 2 + col // NY
    return jnp.where(row == source, 1.0, 0.0).astype(jnp.bfloat16)


def lay_out(source, spread):
    wide = source.astype(jnp.float32)
    count = wide.shape[1] // LANES
    tall = jnp.concatenate(
        [wide[:, r * LANES : (r + 1) * LANES] for r in range(count)], axis=0
    )
    both = jnp.dot(
        tall.astype(jnp.bfloat16), spread, preferred_element_type=jnp.float32
    )
    return both[:, :LANES], both[:, LANES:]


def finish_plane(even, swapped, even_ref, odd_ref, plane):
    lane = lax.broadcasted_iota(jnp.int32, (ROWS * OWN, LANES), 1)
    ahead = jnp.concatenate([swapped[OWN:], swapped[:OWN]], axis=0)
    odd = jnp.where(lane % 2 == 1, ahead, swapped)
    n, p = ROWS * OWN, PAD * OWN
    for ref, value in ((even_ref, even), (odd_ref, odd)):
        ref[plane, p : p + n] = value
        ref[plane, :p] = value[n - p :]
        ref[plane, p + n :] = value[:p]


def put_whole(source, spread, even_ref, odd_ref, plane):
    finish_plane(*lay_out(source, spread), even_ref, odd_ref, plane)


def whole(core, mine, other):
    return jnp.concatenate(
        [jnp.where(core == 0, mine, other), jnp.where(core == 0, other, mine)], axis=1
    )


def add_planes(pairs, phi, orb, acc_in, acc_out, here_plane):
    def tile_step(tile, carry):
        def read(field, z, dx, i):
            refs, plane = field(z)
            start = tile * (8 * OWN) + (PAD + dx // 2) * OWN + i
            return refs[dx % 2][plane, pl.ds(start, 8, stride=OWN), :]

        for z in range(DEPTH):
            if acc_in is None:
                total = [None] * OWN
            else:
                total = [
                    acc_in[z, pl.ds(tile * (8 * OWN) + j, 8, stride=OWN), :]
                    for j in range(OWN)
                ]
            centre = [read(here_plane, z, 0, i) for i in range(OWN)]
            for reach in range(REACH + 1):
                signs = (reach, -reach) if reach else (0,)
                here = [
                    [pltpu.roll(v, 2 * dy % LANES, 1) if dy else v for v in centre]
                    for dy in signs
                ]
                sums = [[None] * OWN for _ in signs]
                rest = REACH - reach
                for dz in range(-rest, rest + 1):
                    if (z, dz) not in pairs:
                        continue
                    for dx in range(abs(dz) - rest, rest - abs(dz) + 1):
                        g = [None for _ in signs]
                        for i in range(OWN):
                            there = read(phi, z + dz, dx, i)
                            for s in range(len(signs)):
                                term = here[s][i] * there
                                g[s] = term if g[s] is None else g[s] + term
                        scale = -WEIGHTS[abs(dx), reach, abs(dz)]
                        g = [v * scale for v in g]
                        for j in range(OWN):
                            there = read(orb, z + dz, dx, j)
                            for s in range(len(signs)):
                                term = g[s] * there
                                old = sums[s][j]
                                sums[s][j] = term if old is None else old + term
                for s, dy in enumerate(signs):
                    for j in range(OWN):
                        term = sums[s][j]
                        if term is None:
                            continue
                        if dy:
                            term = pltpu.roll(term, -2 * dy % LANES, 1)
                        total[j] = term if total[j] is None else total[j] + term
            for j in range(OWN):
                acc_out[z, pl.ds(tile * (8 * OWN) + j, 8, stride=OWN), :] = total[j]
        return carry

    lax.fori_loop(0, ROWS // 8, tile_step, 0)


INSIDE = [
    (z, dz)
    for z in range(DEPTH)
    for dz in range(-REACH, REACH + 1)
    if 0 <= z + dz < DEPTH
]
OUTSIDE = [
    (z, dz)
    for z in range(DEPTH)
    for dz in range(-REACH, REACH + 1)
    if not 0 <= z + dz < DEPTH
]


def kind_of(index):
    return (index ^ (index >> 1) ^ (index >> 3)) & 1


def inner_kernel(mine, other, own, acc, fa, fb, oa, ob):
    spread = spread_matrix()
    kind = kind_of(lax.axis_index("orb"))
    for z in range(DEPTH):
        put_whole(whole(kind, mine[z], other[z]), spread, fa, fb, z)
        put_whole(own[z], spread, oa, ob, z)
    phi = lambda z: ((fa, fb), z)
    orb = lambda z: ((oa, ob), z)
    add_planes(INSIDE, phi, orb, None, acc, phi)


def outer_kernel(
    mine, other, first, second, first_mine, second_mine, first_other, second_other,
    own, acc_in,
    out, part, here, fa, fb, oa, ob, acc,
):
    spread = spread_matrix()
    core = kind_of(lax.axis_index("orb"))
    base = first_is_above(lax.axis_index("orb"), lax.axis_index("dom")) * DEPTH
    rest = DEPTH - base
    for z in range(DEPTH):
        centre = lay_out(whole(core, mine[z], other[z]), spread)[0]
        here[z, PAD * OWN : (PAD + ROWS) * OWN] = centre
        for orbs, halves, plane in (
            (first, (first_mine, first_other), base + z),
            (second, (second_mine, second_other), rest + z),
        ):
            phis = whole(core, halves[0][z], halves[1][z])
            put_whole(orbs[z], spread, oa, ob, plane)
            put_whole(phis, spread, fa, fb, plane)
    plane_of = lambda z: z + DEPTH if z < 0 else z
    phi = lambda z: ((fa, fb), plane_of(z))
    orb = lambda z: ((oa, ob), plane_of(z))
    add_planes(OUTSIDE, phi, orb, acc_in, acc, lambda z: ((here,), z))

    gather = gather_matrix()
    products = None
    for z in range(DEPTH):
        tall = jnp.dot(
            acc[z].astype(jnp.bfloat16), gather, preferred_element_type=jnp.float32
        )
        wide = jnp.concatenate(
            [tall[r * OWN : (r + 1) * OWN] for r in range(ROWS)], axis=1
        ).astype(jnp.bfloat16)
        out[z] = wide
        term = lax.dot_general(
            own[z], wide, (((1,), (1,)), ((), ())), preferred_element_type=jnp.float32
        )
        products = term if products is None else products + term
    part[...] = products


def field(planes):
    return pltpu.VMEM((planes, (ROWS + 2 * PAD) * OWN, LANES), jnp.float32)


SUMS = (DEPTH, ROWS * OWN, LANES)
ON_CHIP = pl.BlockSpec(memory_space=pltpu.VMEM)
PARAMS = pltpu.CompilerParams(vmem_limit_bytes=32 * 1024 * 1024)


def inner(mine, other, own):
    return pl.pallas_call(
        inner_kernel,
        out_shape=jax.ShapeDtypeStruct(SUMS, jnp.float32),
        in_specs=[ON_CHIP] * 3,
        out_specs=ON_CHIP,
        scratch_shapes=[field(DEPTH)] * 4,
        compiler_params=PARAMS,
        cost_estimate=pl.CostEstimate(
            flops=40_000_000, bytes_accessed=1_000_000, transcendentals=0
        ),
    )(mine, other, own)


def outer(*parts):
    return pl.pallas_call(
        outer_kernel,
        out_shape=(
            jax.ShapeDtypeStruct((DEPTH, OWN, ROWS * LANES), jnp.bfloat16),
            jax.ShapeDtypeStruct((OWN, OWN), jnp.float32),
        ),
        in_specs=[ON_CHIP] * 10,
        out_specs=[ON_CHIP] * 2,
        scratch_shapes=[field(DEPTH)]
        + [field(2 * DEPTH)] * 4
        + [pltpu.VMEM(SUMS, jnp.float32)],
        compiler_params=PARAMS,
        cost_estimate=pl.CostEstimate(
            flops=20_000_000, bytes_accessed=2_000_000, transcendentals=0
        ),
    )(*parts)


def swap(x, axis, bits_of):
    size = lax.axis_size(axis)
    return lax.ppermute(x, axis, [(i, i ^ bits_of(i)) for i in range(size)])


def first_is_above(orb, dom):
    return (dom + (orb >> 3)) & 1


def swap_slabs(x):
    axes = ("orb", "dom")
    groups, count = map(lax.axis_size, axes)

    def swap_one(first):
        pairs = []
        for g, s in itertools.product(range(groups), range(count)):
            up = first_is_above(g, s) == first
            target = (s + (1 if up else -1)) % count
            pairs.append((g * count + s, g * count + target))
        return lax.ppermute(x, axes, pairs)

    return swap_one(True), swap_one(False)


def on_device(orbitals, block_owner):
    x = jnp.transpose(orbitals, (1, 0, 2))
    me = lax.axis_index("orb")
    owner = block_owner[0]
    kind = kind_of(me)
    half = x.shape[2] // 2
    cut = lambda v: jnp.where(kind == 0, v[:, :, :half], v[:, :, half:])
    first, second = swap_slabs(x)
    from_mate = swap(x, "orb", lambda i: 1)
    own_half = lax.optimization_barrier(cut(x))
    mine = jnp.where(me == owner, own_half, cut(from_mate))
    known = 1
    for by_kind in ((8, 2), (2, 6), (6, 8)):
        theirs = swap(mine, "orb", lambda i: by_kind[kind_of(i)] ^ 1)
        have = (me ^ owner) & ~known == 0
        mine = jnp.where(have, mine, theirs)
        known = known | jnp.where(kind == 0, by_kind[0], by_kind[1])
    far = swap_slabs(mine)
    other = swap(mine, "orb", lambda i: 1)
    acc = inner(mine, other, x)
    *far, acc, first, second = lax.optimization_barrier((*far, acc, first, second))
    others = [swap(v, "orb", lambda i: 1) for v in far]
    applied, total = outer(mine, other, first, second, *far, *others, x, acc)
    total = lax.all_to_all(
        jnp.broadcast_to(total[None], (lax.axis_size("dom"), OWN, OWN)), "dom", 0, 0
    ).sum(0)
    return jnp.transpose(applied, (1, 0, 2)), total / 512.0


def solution(mesh):
    in_specs = (P("orb", "dom", None), P())
    out_specs = (P("orb", "dom", None), P("orb", None))
    return jax.shard_map(
        on_device, mesh=mesh, in_specs=in_specs, out_specs=out_specs, check_vma=False
    )
```

```python
import itertools

import jax
import jax.numpy as jnp
from jax import lax
from jax.experimental import pallas as pl
from jax.experimental.pallas import tpu as pltpu
from jax.sharding import PartitionSpec as P

NY = 64
OWN = 8
LANES = 128
CELLS = 4096
ROWS = 32
PAD = 2
DEPTH = 3
REACH = 3

C = 1.0 / 6.02


def weight(dx, dy, dz):
    steps = ((1, 0, 0), (-1, 0, 0), (0, 1, 0), (0, -1, 0), (0, 0, 1), (0, 0, -1))
    total = 0.0
    for length in range(REACH + 1):
        walks = sum(
            tuple(map(sum, zip((0, 0, 0), *walk))) == (dx, dy, dz)
            for walk in itertools.product(steps, repeat=length)
        )
        total += walks * C ** (length + 1)
    return total


WEIGHTS = {
    d: weight(*d)
    for d in itertools.product(range(REACH + 1), repeat=3)
    if sum(d) <= REACH
}


def spread_matrix():
    row = lax.broadcasted_iota(jnp.int32, (LANES, 2 * LANES), 0)
    col = lax.broadcasted_iota(jnp.int32, (LANES, 2 * LANES), 1)
    half = col // LANES
    lane = col % LANES
    source = (lane % 2 + half) % 2 * NY + lane // 2
    return jnp.where(row == source, 1.0, 0.0).astype(jnp.bfloat16)


def gather_matrix():
    row = lax.broadcasted_iota(jnp.int32, (LANES, LANES), 0)
    col = lax.broadcasted_iota(jnp.int32, (LANES, LANES), 1)
    source = col % NY * 2 + col // NY
    return jnp.where(row == source, 1.0, 0.0).astype(jnp.bfloat16)


def lay_out(source, spread):
    wide = source.astype(jnp.float32)
    count = wide.shape[1] // LANES
    tall = jnp.concatenate(
        [wide[:, r * LANES : (r + 1) * LANES] for r in range(count)], axis=0
    )
    both = jnp.dot(
        tall.astype(jnp.bfloat16), spread, preferred_element_type=jnp.float32
    )
    return both[:, :LANES], both[:, LANES:]


def finish_plane(even, swapped, even_ref, odd_ref, plane):
    lane = lax.broadcasted_iota(jnp.int32, (ROWS * OWN, LANES), 1)
    ahead = jnp.concatenate([swapped[OWN:], swapped[:OWN]], axis=0)
    odd = jnp.where(lane % 2 == 1, ahead, swapped)
    n, p = ROWS * OWN, PAD * OWN
    for ref, value in ((even_ref, even), (odd_ref, odd)):
        ref[plane, p : p + n] = value
        ref[plane, :p] = value[n - p :]
        ref[plane, p + n :] = value[:p]


def put_whole(source, spread, even_ref, odd_ref, plane):
    finish_plane(*lay_out(source, spread), even_ref, odd_ref, plane)


def whole(core, mine, other):
    return jnp.concatenate(
        [jnp.where(core == 0, mine, other), jnp.where(core == 0, other, mine)], axis=1
    )


def add_planes(pairs, phi, orb, acc_in, acc_out, here_plane):
    def tile_step(tile, carry):
        def read(field, z, dx, i):
            refs, plane = field(z)
            start = tile * (8 * OWN) + (PAD + dx // 2) * OWN + i
            return refs[dx % 2][plane, pl.ds(start, 8, stride=OWN), :]

        for z in range(DEPTH):
            if acc_in is None:
                total = [None] * OWN
            else:
                total = [
                    acc_in[z, pl.ds(tile * (8 * OWN) + j, 8, stride=OWN), :]
                    for j in range(OWN)
                ]
            centre = [read(here_plane, z, 0, i) for i in range(OWN)]
            for reach in range(REACH + 1):
                signs = (reach, -reach) if reach else (0,)
                here = [
                    [pltpu.roll(v, 2 * dy % LANES, 1) if dy else v for v in centre]
                    for dy in signs
                ]
                sums = [[None] * OWN for _ in signs]
                rest = REACH - reach
                for dz in range(-rest, rest + 1):
                    if (z, dz) not in pairs:
                        continue
                    for dx in range(abs(dz) - rest, rest - abs(dz) + 1):
                        g = [None for _ in signs]
                        for i in range(OWN):
                            there = read(phi, z + dz, dx, i)
                            for s in range(len(signs)):
                                term = here[s][i] * there
                                g[s] = term if g[s] is None else g[s] + term
                        scale = -WEIGHTS[abs(dx), reach, abs(dz)]
                        g = [v * scale for v in g]
                        for j in range(OWN):
                            there = read(orb, z + dz, dx, j)
                            for s in range(len(signs)):
                                term = g[s] * there
                                old = sums[s][j]
                                sums[s][j] = term if old is None else old + term
                for s, dy in enumerate(signs):
                    for j in range(OWN):
                        term = sums[s][j]
                        if term is None:
                            continue
                        if dy:
                            term = pltpu.roll(term, -2 * dy % LANES, 1)
                        total[j] = term if total[j] is None else total[j] + term
            for j in range(OWN):
                acc_out[z, pl.ds(tile * (8 * OWN) + j, 8, stride=OWN), :] = total[j]
        return carry

    lax.fori_loop(0, ROWS // 8, tile_step, 0, unroll=acc_in is not None)


INSIDE = [
    (z, dz)
    for z in range(DEPTH)
    for dz in range(-REACH, REACH + 1)
    if 0 <= z + dz < DEPTH
]
OUTSIDE = [
    (z, dz)
    for z in range(DEPTH)
    for dz in range(-REACH, REACH + 1)
    if not 0 <= z + dz < DEPTH
]


def kind_of(index):
    return (index ^ (index >> 1) ^ (index >> 3)) & 1


def inner_kernel(mine, other, own, acc, fa, fb, oa, ob):
    spread = spread_matrix()
    kind = kind_of(lax.axis_index("orb"))
    for z in range(DEPTH):
        put_whole(whole(kind, mine[z], other[z]), spread, fa, fb, z)
        put_whole(own[z], spread, oa, ob, z)
    phi = lambda z: ((fa, fb), z)
    orb = lambda z: ((oa, ob), z)
    add_planes(INSIDE, phi, orb, None, acc, phi)


def outer_kernel(
    mine, other, first, second, first_mine, second_mine, first_other, second_other,
    own, acc_in,
    out, part, here, fa, fb, oa, ob, acc,
):
    spread = spread_matrix()
    core = kind_of(lax.axis_index("orb"))
    base = first_is_above(lax.axis_index("orb"), lax.axis_index("dom")) * DEPTH
    rest = DEPTH - base
    for z in range(DEPTH):
        centre = lay_out(whole(core, mine[z], other[z]), spread)[0]
        here[z, PAD * OWN : (PAD + ROWS) * OWN] = centre
        for orbs, halves, plane in (
            (first, (first_mine, first_other), base + z),
            (second, (second_mine, second_other), rest + z),
        ):
            phis = whole(core, halves[0][z], halves[1][z])
            put_whole(orbs[z], spread, oa, ob, plane)
            put_whole(phis, spread, fa, fb, plane)
    plane_of = lambda z: z + DEPTH if z < 0 else z
    phi = lambda z: ((fa, fb), plane_of(z))
    orb = lambda z: ((oa, ob), plane_of(z))
    add_planes(OUTSIDE, phi, orb, acc_in, acc, lambda z: ((here,), z))

    gather = gather_matrix()
    products = None
    for z in range(DEPTH):
        tall = jnp.dot(
            acc[z].astype(jnp.bfloat16), gather, preferred_element_type=jnp.float32
        )
        wide = jnp.concatenate(
            [tall[r * OWN : (r + 1) * OWN] for r in range(ROWS)], axis=1
        ).astype(jnp.bfloat16)
        out[z] = wide
        term = lax.dot_general(
            own[z], wide, (((1,), (1,)), ((), ())), preferred_element_type=jnp.float32
        )
        products = term if products is None else products + term
    part[...] = products


def field(planes):
    return pltpu.VMEM((planes, (ROWS + 2 * PAD) * OWN, LANES), jnp.float32)


SUMS = (DEPTH, ROWS * OWN, LANES)
ON_CHIP = pl.BlockSpec(memory_space=pltpu.VMEM)
PARAMS = pltpu.CompilerParams(vmem_limit_bytes=32 * 1024 * 1024)


def inner(mine, other, own):
    return pl.pallas_call(
        inner_kernel,
        out_shape=jax.ShapeDtypeStruct(SUMS, jnp.float32),
        in_specs=[ON_CHIP] * 3,
        out_specs=ON_CHIP,
        scratch_shapes=[field(DEPTH)] * 4,
        compiler_params=PARAMS,
        cost_estimate=pl.CostEstimate(
            flops=40_000_000, bytes_accessed=1_000_000, transcendentals=0
        ),
    )(mine, other, own)


def outer(*parts):
    return pl.pallas_call(
        outer_kernel,
        out_shape=(
            jax.ShapeDtypeStruct((DEPTH, OWN, ROWS * LANES), jnp.bfloat16),
            jax.ShapeDtypeStruct((OWN, OWN), jnp.float32),
        ),
        in_specs=[ON_CHIP] * 10,
        out_specs=[ON_CHIP] * 2,
        scratch_shapes=[field(DEPTH)]
        + [field(2 * DEPTH)] * 4
        + [pltpu.VMEM(SUMS, jnp.float32)],
        compiler_params=PARAMS,
        cost_estimate=pl.CostEstimate(
            flops=20_000_000, bytes_accessed=2_000_000, transcendentals=0
        ),
    )(*parts)


def swap(x, axis, bits_of):
    size = lax.axis_size(axis)
    return lax.ppermute(x, axis, [(i, i ^ bits_of(i)) for i in range(size)])


def first_is_above(orb, dom):
    return (dom + (orb >> 3)) & 1


def swap_slabs(x):
    axes = ("orb", "dom")
    groups, count = map(lax.axis_size, axes)

    def swap_one(first):
        pairs = []
        for g, s in itertools.product(range(groups), range(count)):
            up = first_is_above(g, s) == first
            target = (s + (1 if up else -1)) % count
            pairs.append((g * count + s, g * count + target))
        return lax.ppermute(x, axes, pairs)

    return swap_one(True), swap_one(False)


def on_device(orbitals, block_owner):
    x = jnp.transpose(orbitals, (1, 0, 2))
    me = lax.axis_index("orb")
    owner = block_owner[0]
    kind = kind_of(me)
    half = x.shape[2] // 2
    cut = lambda v: jnp.where(kind == 0, v[:, :, :half], v[:, :, half:])
    first, second = swap_slabs(x)
    from_mate = swap(x, "orb", lambda i: 1)
    own_half = lax.optimization_barrier(cut(x))
    mine = jnp.where(me == owner, own_half, cut(from_mate))
    known = 1
    for by_kind in ((8, 2), (2, 6), (6, 8)):
        theirs = swap(mine, "orb", lambda i: by_kind[kind_of(i)] ^ 1)
        have = (me ^ owner) & ~known == 0
        mine = jnp.where(have, mine, theirs)
        known = known | jnp.where(kind == 0, by_kind[0], by_kind[1])
    far = swap_slabs(mine)
    other = swap(mine, "orb", lambda i: 1)
    acc = inner(mine, other, x)
    *far, acc, first, second = lax.optimization_barrier((*far, acc, first, second))
    others = [swap(v, "orb", lambda i: 1) for v in far]
    applied, total = outer(mine, other, first, second, *far, *others, x, acc)
    total = lax.all_to_all(
        jnp.broadcast_to(total[None], (lax.axis_size("dom"), OWN, OWN)), "dom", 0, 0
    ).sum(0)
    return jnp.transpose(applied, (1, 0, 2)), total / 512.0


def solution(mesh):
    in_specs = (P("orb", "dom", None), P())
    out_specs = (P("orb", "dom", None), P("orb", None))
    return jax.shard_map(
        on_device, mesh=mesh, in_specs=in_specs, out_specs=out_specs, check_vma=False
    )
```
